128 devices in a mesh: seq: 8 (over y, z_hi), blk: 16 (over z_lo, x, core).
Axes of the slice: x: 4, y: 4, z: 4 (z_hi: 2, z_lo: 2; z = z_hi * 2 + z_lo), core: 2. Of those that a mesh axis runs over, the one named last changes fastest.
Arguments:
- queries: bfloat16 [8192, 8192], P(('seq', 'blk')), may hold values from -72 to 72
- keys: bfloat16 [8192, 1024], P(('seq', 'blk')), may hold values from -6 to 6
- values: bfloat16 [8192, 1024], P(('seq', 'blk')), may hold values from -8 to 8
Outputs:
- attended: bfloat16 [8192, 8192], P(('seq', 'blk'))
The draws below stay inside these ranges and needn't reach their ends.
All inputs are finite; a program needn't handle non-finite values.
Results may differ from the reference program's by a relative error of at most 0.012.
Values may be sent and summed in bfloat16 or wider, within the bound.
No kernel may reach another device: no remote copies, remote signals or barrier semaphores. Data moves between devices by JAX's collectives and lax.ppermute only.
A program may use at most 128 MiB of HBM per device.

```python
import math
import jax
import jax.numpy as jnp
from jax import lax

HEADS_Q = 64
HEADS_KV = 8
HEAD_DIM = 128
LENGTH = 8192


def draw_queries(key, part):
    key = jax.random.fold_in(key, 1)
    noise_key = jax.random.fold_in(key, 0)
    base = jax.random.normal(noise_key, (LENGTH, HEADS_Q * HEAD_DIM), jnp.float32)
    base = jnp.clip(base, -6.0, 6.0)
    return base.astype(jnp.bfloat16)


def draw_keys(key, part):
    key = jax.random.fold_in(key, 2)
    noise_key = jax.random.fold_in(key, 0)
    base = jax.random.normal(noise_key, (LENGTH, HEADS_KV * HEAD_DIM), jnp.float32)
    base = jnp.clip(base, -6.0, 6.0)
    return base.astype(jnp.bfloat16)


def draw_values(key, part):
    key = jax.random.fold_in(key, 3)
    noise_key, offset_key = jax.random.split(key)
    base = jax.random.normal(noise_key, (LENGTH, HEADS_KV * HEAD_DIM), jnp.float32)
    shift_amounts = jax.random.normal(offset_key, (LENGTH // 16, HEADS_KV * HEAD_DIM), jnp.float32)
    whole = base + jnp.repeat(shift_amounts, 16, axis=0)
    return jnp.clip(whole, -8.0, 8.0).astype(jnp.bfloat16)


def setup_inputs(seed: int = 0) -> dict:
    key_list = jax.random.split(jax.random.key(seed), 4)
    return {
        "queries": draw_queries(jax.random.fold_in(key_list[3], 71), 0),
        "keys": draw_keys(jax.random.fold_in(key_list[3], 71), 0),
        "values": draw_values(jax.random.fold_in(key_list[3], 71), 0),
    }


def sylvester(order_size):
    indices = jnp.arange(order_size, dtype=jnp.int32)
    parity = jnp.zeros((order_size, order_size), jnp.int32)
    for bit_pos in range(order_size.bit_length() - 1):
        parity = parity + ((indices[:, None] >> bit_pos) & 1) * ((indices[None, :] >> bit_pos) & 1)
    return (1 - 2 * (parity % 2)).astype(jnp.bfloat16)


def rotate(matrix, order_size):
    head_count = matrix.shape[1] // order_size
    flattened = matrix.reshape(matrix.shape[0] * head_count, order_size)
    turned = jnp.dot(flattened, sylvester(order_size), preferred_element_type=jnp.float32) * (order_size ** -0.5)
    return turned.astype(jnp.bfloat16).reshape(matrix.shape)


def reference(queries, keys, values):
    rotated_keys = lax.optimization_barrier(rotate(keys, HEAD_DIM))
    rotated_values = lax.optimization_barrier(rotate(values, HEAD_DIM))
    group_size = HEADS_Q // HEADS_KV
    block_rows = math.gcd(LENGTH, 512)
    query_group_count = queries.reshape(LENGTH, HEADS_KV, group_size, HEAD_DIM)
    key_heads = rotated_keys.reshape(LENGTH, HEADS_KV, HEAD_DIM)
    value_heads = rotated_values.reshape(LENGTH, HEADS_KV, HEAD_DIM)
    positions = jnp.arange(LENGTH, dtype=jnp.int32)

    def one_head(head):
        key_tensor = lax.dynamic_index_in_dim(key_heads, head, 1, keepdims=False).astype(jnp.float32)
        value_matrix = lax.dynamic_index_in_dim(value_heads, head, 1, keepdims=False).astype(jnp.float32)
        query_matrix = lax.dynamic_index_in_dim(query_group_count, head, 1, keepdims=False)

        def one_block(block):
            first_row = block * block_rows
            block_of_queries = lax.dynamic_slice_in_dim(query_matrix, first_row, block_rows, 0).astype(jnp.float32)
            scores = jnp.einsum("qgd,kd->qgk", block_of_queries, key_tensor) * (HEAD_DIM ** -0.5)
            query_pos = first_row + jnp.arange(block_rows, dtype=jnp.int32)
            visible = positions[None, :] <= query_pos[:, None]
            scores = jnp.where(visible[:, None, :], scores, -jnp.inf)
            weights = jnp.exp(scores - jnp.max(scores, axis=-1, keepdims=True))
            totals = jnp.sum(weights, axis=-1)
            rounded = lax.optimization_barrier(weights.astype(jnp.bfloat16)).astype(jnp.float32)
            output = jnp.einsum("qgk,kd->qgd", rounded, value_matrix) / totals[..., None]
            return output.astype(jnp.bfloat16)

        blocks_out = lax.map(one_block, jnp.arange(LENGTH // block_rows, dtype=jnp.int32))
        return blocks_out.reshape(LENGTH, group_size, HEAD_DIM)

    heads_out = lax.map(one_head, jnp.arange(HEADS_KV, dtype=jnp.int32))
    return jnp.transpose(heads_out, (1, 0, 2, 3)).reshape(LENGTH, HEADS_Q * HEAD_DIM)
```

```python
import functools
import math

import jax
import jax.numpy as jnp
from jax import lax
from jax.experimental import pallas as pl
from jax.experimental.pallas import tpu as pltpu
from jax.sharding import Mesh, PartitionSpec as P

HEAD_DIM = 128
GROUP = 8
TOK = 64
AXES = ("y", "zh", "zl", "x", "core")
SIZES = (4, 2, 2, 4, 2)
HEADS_OVER = ("y", "zl")
COPIES_OVER = ("y", "zh", "zl")
CHUNK = GROUP * TOK
PAIR = 2 * CHUNK
STEP = 256
EARLY = 6
SCALE_LOG2 = HEAD_DIM ** (-0.5) * math.log2(math.e)
LOW, HIGH = 2.0**-60, 2.0**100
HIDDEN = -1e30
VMEM = pl.BlockSpec(memory_space=pltpu.VMEM)


def prepare_kernel(k_ref, v_ref, kv_ref):
    i = lax.broadcasted_iota(jnp.int32, (HEAD_DIM, HEAD_DIM), 0)
    j = lax.broadcasted_iota(jnp.int32, (HEAD_DIM, HEAD_DIM), 1)
    parity = i & j
    for shift in (4, 2, 1):
        parity = parity ^ (parity >> shift)
    matrix = (1 - 2 * (parity & 1)).astype(jnp.float32).astype(jnp.bfloat16)
    for part, ref in enumerate((k_ref, v_ref)):
        for h in range(ref.shape[1] // HEAD_DIM):
            turned = jnp.dot(
                ref[:, h * HEAD_DIM : (h + 1) * HEAD_DIM], matrix, preferred_element_type=jnp.float32
            ) * HEAD_DIM ** (-0.5)
            for zh in range(2):
                kv_ref[h // 2, zh, h % 2, part] = turned.astype(jnp.bfloat16)


def prepare(keys, values):
    return pl.pallas_call(
        prepare_kernel,
        out_shape=jax.ShapeDtypeStruct((4, 2, 2, 2, TOK, HEAD_DIM), jnp.bfloat16),
    )(keys, values)


class Tiles:
    def __init__(self, where_ref, first_slot, q_ref, acc_ref, block_refs, bias_ref):
        self.q, self.acc, self.blocks, self.bias = q_ref, acc_ref, block_refs, bias_ref
        self.zh = where_ref[0]
        token = lax.broadcasted_iota(jnp.int32, (TOK, TOK), 0)
        key = lax.broadcasted_iota(jnp.int32, (TOK, TOK), 1)
        for b in range(len(block_refs)):
            ahead = where_ref[2 + first_slot + b] - where_ref[1]
            bias_ref[:, b * TOK : (b + 1) * TOK] = jnp.where(ahead * TOK + key <= token, 0.0, HIDDEN)

    def load(self, part, quads):
        return jnp.concatenate([r[(*quad, part)] for quad in quads for r in self.blocks], axis=0)

    def scores(self, y, row, rows, quads, masked):
        x = (
            lax.dot_general(
                self.q[y, pl.ds(row, rows), :],
                self.load(0, quads),
                (((1,), (1,)), ((), ())),
                preferred_element_type=jnp.float32,
            )
            * SCALE_LOG2
        )
        if masked:
            seen = x.shape[1] - self.bias.shape[1]
            hidden = x[:, seen:] + jnp.concatenate([self.bias[...]] * (rows // TOK), axis=0)
            x = jnp.concatenate([x[:, :seen], hidden], axis=1) if seen else hidden
        return x

    def weigh(self, weights, quads):
        values = self.load(1, quads)
        return jnp.dot(
            weights.astype(jnp.bfloat16),
            jnp.concatenate([values, jnp.ones_like(values)], axis=1),
            preferred_element_type=jnp.float32,
        )

    def run(self, y, jobs, fresh):
        x = None
        for n, (row, quads, masked) in enumerate(jobs):
            if x is None:
                x = self.scores(y, row, STEP, quads, masked)
            weights = jnp.exp2(x)
            if n + 1 < len(jobs):
                x = self.scores(y, jobs[n + 1][0], STEP, *jobs[n + 1][1:])
            out = self.weigh(weights, quads)
            at = (y, pl.ds(row, STEP), slice(None))
            self.acc[at] = out if fresh else self.acc[at] + out

    def same_y(self, y, fresh):
        def jobs(others):
            listed = []
            for row in range(0, PAIR, STEP):
                own = [(y, self.zh, zl) for zl in range(row // CHUNK + 1)]
                listed.append((row, others + own, True))
            return listed

        @pl.when(self.zh == 1)
        def _():
            self.run(y, jobs([(y, 0, 0), (y, 0, 1)]), fresh)

        @pl.when(self.zh == 0)
        def _():
            self.run(y, jobs([]), fresh)

    def earlier_y(self, y):
        def one(key_y, carry):
            quads = [(key_y, zh, zl) for zh in range(2) for zl in range(2)]
            self.run(y, [(row, quads, False) for row in range(0, PAIR, STEP)], False)
            return carry

        lax.fori_loop(0, y, one, 0)


def first_kernel(*refs):
    where_ref, q_ref = refs[:2]
    block_refs = refs[2 : 2 + EARLY]
    acc_ref, bias_ref = refs[2 + EARLY :]
    tiles = Tiles(where_ref, 0, q_ref, acc_ref, block_refs, bias_ref)

    def pair(y, carry):
        tiles.same_y(y, True)
        tiles.earlier_y(y)
        return carry

    lax.fori_loop(0, 4, pair, 0)


def last_kernel(*refs):
    where_ref, q_ref, before_ref = refs[:3]
    block_refs = refs[3:11]
    o_ref, acc, bias, full_bias, top = refs[11:]
    tiles = Tiles(where_ref, EARLY, q_ref, acc, block_refs[EARLY:], bias)

    def pair(y, bad):
        acc[y] = before_ref[y]
        tiles.same_y(y, False)
        tiles.earlier_y(y)
        total = acc[y, :, HEAD_DIM:]
        o_ref[y] = (acc[y, :, :HEAD_DIM] / total).astype(jnp.bfloat16)
        fine = (total >= LOW) & (total <= HIGH)
        return jnp.maximum(bad, jnp.max(jnp.where(fine, 0.0, 1.0)))

    bad = lax.fori_loop(0, 4, pair, jnp.float32(0.0))

    @pl.when(bad > 0.0)
    def _():
        every = Tiles(where_ref, 0, q_ref, acc, block_refs, full_bias)

        def exact(y, zl, quad, first, masked):
            row = pl.multiple_of(zl * CHUNK, CHUNK)
            rows = pl.ds(row, CHUNK)
            x = every.scores(y, row, CHUNK, [quad], masked)
            high = jnp.max(x, axis=1, keepdims=True)
            if first:
                acc[y, rows, :] = every.weigh(jnp.exp2(x - high), [quad])
            else:
                before = top[:, :1]
                high = jnp.maximum(high, before)
                acc[y, rows, :] = acc[y, rows, :] * jnp.exp2(before - high) + every.weigh(
                    jnp.exp2(x - high), [quad]
                )
            top[...] = jnp.broadcast_to(high, top.shape)

        def exact_chunk(n, carry):
            y, zl = n // 2, n % 2
            exact(y, zl, (y, every.zh, zl), True, True)
            own = 4 * y + 2 * every.zh + zl

            def others(m, carry):
                exact(y, zl, (m // 4, m // 2 % 2, m % 2), False, False)
                return carry

            lax.fori_loop(0, own, others, 0)
            rows = pl.ds(pl.multiple_of(zl * CHUNK, CHUNK), CHUNK)
            o_ref[y, rows, :] = (acc[y, rows, :HEAD_DIM] / acc[y, rows, HEAD_DIM:]).astype(jnp.bfloat16)
            return carry

        lax.fori_loop(0, 8, exact_chunk, 0)


def cost(share):
    return pl.CostEstimate(
        flops=int(20e9 * share), bytes_accessed=6 * 2**20, transcendentals=int(2e7 * share)
    )


def attend_first(where, queries, blocks):
    return pl.pallas_call(
        first_kernel,
        out_shape=jax.ShapeDtypeStruct((4, PAIR, 2 * HEAD_DIM), jnp.float32),
        in_specs=[pl.BlockSpec(memory_space=pltpu.SMEM)] + [VMEM] * (1 + EARLY),
        out_specs=VMEM,
        scratch_shapes=[pltpu.VMEM((TOK, EARLY * TOK), jnp.float32)],
        compiler_params=pltpu.CompilerParams(vmem_limit_bytes=36 * 2**20),
        cost_estimate=cost(EARLY / 8),
    )(where, queries, *blocks)


def attend_last(where, queries, before, blocks):
    return pl.pallas_call(
        last_kernel,
        out_shape=jax.ShapeDtypeStruct((4, PAIR, HEAD_DIM), jnp.bfloat16),
        in_specs=[pl.BlockSpec(memory_space=pltpu.SMEM)] + [VMEM] * 10,
        out_specs=VMEM,
        scratch_shapes=[
            pltpu.VMEM((4, PAIR, 2 * HEAD_DIM), jnp.float32),
            pltpu.VMEM((TOK, (8 - EARLY) * TOK), jnp.float32),
            pltpu.VMEM((TOK, 8 * TOK), jnp.float32),
            pltpu.VMEM((CHUNK, HEAD_DIM), jnp.float32),
        ],
        compiler_params=pltpu.CompilerParams(vmem_limit_bytes=36 * 2**20),
        cost_estimate=cost(1 - EARLY / 8),
    )(where, queries, before, *blocks)


def fetch(array, axis, step):
    size = SIZES[AXES.index(axis)]
    return lax.ppermute(array, axis, [((n + step) % size, n) for n in range(size)])


def on_device(queries, keys, values):
    zh, x, core = (lax.axis_index(a) for a in ("zh", "x", "core"))
    kv = prepare(keys, values).reshape(16, 2, TOK, HEAD_DIM)
    own = lax.all_to_all(kv, COPIES_OVER, split_axis=0, concat_axis=0, tiled=True)
    own = own.reshape(4, 2, 2, 2, TOK, HEAD_DIM)
    q = queries.reshape(TOK, 8 * GROUP, HEAD_DIM).transpose(1, 0, 2).reshape(8, CHUNK, HEAD_DIM)
    q, _ = lax.optimization_barrier((q, own))
    q = lax.all_to_all(q, HEADS_OVER, split_axis=0, concat_axis=0, tiled=True)
    q = q.reshape(4, PAIR, HEAD_DIM)
    blocks, slots = [], []
    for step in (0, 1, 3, 2):
        block = fetch(own, "x", step) if step else own
        blocks += [block, fetch(block, "core", 1)]
        slots += [(x + step) % 4 * 2 + core, (x + step) % 4 * 2 + 1 - core]
    where = jnp.stack([zh, x * 2 + core] + slots).astype(jnp.int32)
    acc = attend_first(where, q, blocks[:EARLY])
    out = attend_last(where, q, acc, blocks).reshape(8, CHUNK, HEAD_DIM)
    out = lax.all_to_all(out, HEADS_OVER, split_axis=0, concat_axis=0, tiled=True)
    return out.reshape(8 * GROUP, TOK, HEAD_DIM).transpose(1, 0, 2).reshape(queries.shape)


def solution(mesh):
    fine = Mesh(mesh.devices.reshape(SIZES), AXES)
    spec = P(AXES, None)
    return jax.shard_map(
        on_device, mesh=fine, in_specs=(spec,) * 3, out_specs=spec, check_vma=False
    )
```

```python
import math

import jax
import jax.numpy as jnp
from jax import lax
from jax.experimental import pallas as pl
from jax.experimental.pallas import tpu as pltpu
from jax.sharding import Mesh, PartitionSpec as P

HEAD_DIM = 128
GROUP = 8
TOK = 64
SIZES = {"yz": 16, "xc": 8}
TRADERS = [[4 * y + z for y in range(4) for z in zs] for zs in ((0, 3), (1, 2))]
CHUNK = GROUP * TOK
PAIR = 2 * CHUNK
STEP = 256
SCALE_LOG2 = HEAD_DIM ** (-0.5) * math.log2(math.e)
LOW, HIGH = 2.0**-60, 2.0**100
HIDDEN = -1e30
VMEM = pl.BlockSpec(memory_space=pltpu.VMEM)


def prepare_kernel(k_ref, v_ref, kv_ref):
    i = lax.broadcasted_iota(jnp.int32, (HEAD_DIM, HEAD_DIM), 0)
    j = lax.broadcasted_iota(jnp.int32, (HEAD_DIM, HEAD_DIM), 1)
    parity = i & j
    for shift in (4, 2, 1):
        parity = parity ^ (parity >> shift)
    matrix = (1 - 2 * (parity & 1)).astype(jnp.float32).astype(jnp.bfloat16)
    heads = k_ref.shape[1] // HEAD_DIM
    for part, ref in enumerate((k_ref, v_ref)):
        rows = jnp.concatenate([ref[:, h * HEAD_DIM : (h + 1) * HEAD_DIM] for h in range(heads)], axis=0)
        turned = jnp.dot(rows, matrix, preferred_element_type=jnp.float32) * HEAD_DIM ** (-0.5)
        turned = turned.astype(jnp.bfloat16)
        for h in range(heads):
            for n in range(2):
                kv_ref[2 * h + n, part] = turned[h * TOK : (h + 1) * TOK]


def prepare(keys, values):
    return pl.pallas_call(
        prepare_kernel,
        out_shape=jax.ShapeDtypeStruct((16, 2, TOK, HEAD_DIM), jnp.bfloat16),
    )(keys, values)


def by_head_kernel(q_ref, o_ref):
    for h in range(o_ref.shape[0]):
        o_ref[h] = q_ref[:, h * HEAD_DIM : (h + 1) * HEAD_DIM]


def by_head(queries):
    heads = queries.shape[1] // HEAD_DIM
    return pl.pallas_call(
        by_head_kernel,
        out_shape=jax.ShapeDtypeStruct((heads, TOK, HEAD_DIM), jnp.bfloat16),
    )(queries)


def after_kernel(array_ref, token_ref, o_ref):
    del array_ref, token_ref, o_ref


def after(array, token):
    return pl.pallas_call(
        after_kernel,
        out_shape=jax.ShapeDtypeStruct(array.shape, array.dtype),
        in_specs=[pl.BlockSpec(memory_space=pl.ANY)] * 2,
        out_specs=pl.BlockSpec(memory_space=pl.ANY),
        input_output_aliases={0: 0},
        cost_estimate=pl.CostEstimate(flops=5 * 10**9, bytes_accessed=0, transcendentals=0),
    )(array, token)


def attend_kernel(*refs):
    where_ref, q_ref = refs[:2]
    block_refs = refs[2:10]
    o_ref, acc, bias, top = refs[10:]
    inner = where_ref[0]
    token = lax.broadcasted_iota(jnp.int32, (TOK, TOK), 0)
    key = lax.broadcasted_iota(jnp.int32, (TOK, TOK), 1)
    for b in range(8):
        ahead = where_ref[2 + b] - where_ref[1]
        bias[:, b * TOK : (b + 1) * TOK] = jnp.where(ahead * TOK + key <= token, 0.0, HIDDEN)

    def load(part, quads):
        return jnp.concatenate([r[(*quad, part)] for quad in quads for r in block_refs], axis=0)

    def scores(y, row, rows, quads, masked):
        x = (
            lax.dot_general(
                q_ref[y, pl.ds(row, rows), :],
                load(0, quads),
                (((1,), (1,)), ((), ())),
                preferred_element_type=jnp.float32,
            )
            * SCALE_LOG2
        )
        if masked:
            seen = x.shape[1] - bias.shape[1]
            hidden = x[:, seen:] + jnp.concatenate([bias[...]] * (rows // TOK), axis=0)
            x = jnp.concatenate([x[:, :seen], hidden], axis=1) if seen else hidden
        return x

    def weigh(weights, quads):
        values = load(1, quads)
        return jnp.dot(
            weights.astype(jnp.bfloat16),
            jnp.concatenate([values, jnp.ones_like(values)], axis=1),
            preferred_element_type=jnp.float32,
        )

    def run(y, jobs, fresh):
        x = scores(y, jobs[0][0], STEP, *jobs[0][1:])
        for n, (row, quads, _) in enumerate(jobs):
            weights = jnp.exp2(x)
            if n + 1 < len(jobs):
                x = scores(y, jobs[n + 1][0], STEP, *jobs[n + 1][1:])
            out = weigh(weights, quads)
            at = pl.ds(row, STEP)
            acc[at, :] = out if fresh else acc[at, :] + out

    def same_y(y, zs):
        jobs = [
            (row, [(y, z) for z in range(zs[row // CHUNK] + 1)], True) for row in range(0, PAIR, STEP)
        ]
        run(y, jobs, True)

    def store(y, m):
        rows = slice(m * CHUNK, (m + 1) * CHUNK)
        out = (acc[rows, :HEAD_DIM] / acc[rows, HEAD_DIM:]).astype(jnp.bfloat16)
        for h in range(GROUP):
            o_ref[2 * y + m, :, h * HEAD_DIM : (h + 1) * HEAD_DIM] = out[h * TOK : (h + 1) * TOK]

    def pair(y, bad):
        pl.when(inner == 0)(lambda: same_y(y, (0, 3)))
        pl.when(inner == 1)(lambda: same_y(y, (1, 2)))

        def earlier(key_y, carry):
            quads = [(key_y, z) for z in range(4)]
            run(y, [(row, quads, False) for row in range(0, PAIR, STEP)], False)
            return carry

        lax.fori_loop(0, y, earlier, 0)
        total = acc[:, HEAD_DIM:]
        for m in range(2):
            store(y, m)
        fine = (total >= LOW) & (total <= HIGH)
        return jnp.maximum(bad, jnp.max(jnp.where(fine, 0.0, 1.0)))

    bad = lax.fori_loop(0, 4, pair, jnp.float32(0.0))

    @pl.when(bad > 0.0)
    def _():
        def exact(y, m, quad, first):
            row = pl.multiple_of(m * CHUNK, CHUNK)
            rows = pl.ds(row, CHUNK)
            x = scores(y, row, CHUNK, [quad], first)
            high = jnp.max(x, axis=1, keepdims=True)
            if first:
                acc[rows, :] = weigh(jnp.exp2(x - high), [quad])
            else:
                before = top[:, :1]
                high = jnp.maximum(high, before)
                acc[rows, :] = acc[rows, :] * jnp.exp2(before - high) + weigh(jnp.exp2(x - high), [quad])
            top[...] = jnp.broadcast_to(high, top.shape)

        def exact_chunk(n, m):
            z = inner + m * (3 - 2 * inner)
            exact(n, m, (n, z), True)

            def others(k, carry):
                exact(n, m, (k // 4, k % 4), False)
                return carry

            lax.fori_loop(0, 4 * n + z, others, 0)
            store(n, m)

        def exact_pair(y, carry):
            for m in range(2):
                exact_chunk(y, m)
            return carry

        lax.fori_loop(0, 4, exact_pair, 0)


def attend(where, queries, blocks):
    return pl.pallas_call(
        attend_kernel,
        out_shape=jax.ShapeDtypeStruct((8, TOK, GROUP * HEAD_DIM), jnp.bfloat16),
        in_specs=[pl.BlockSpec(memory_space=pltpu.SMEM)] + [VMEM] * 9,
        out_specs=VMEM,
        scratch_shapes=[
            pltpu.VMEM((PAIR, 2 * HEAD_DIM), jnp.float32),
            pltpu.VMEM((TOK, 8 * TOK), jnp.float32),
            pltpu.VMEM((CHUNK, HEAD_DIM), jnp.float32),
        ],
        compiler_params=pltpu.CompilerParams(vmem_limit_bytes=20 * 2**20),
        cost_estimate=pl.CostEstimate(flops=2 * 10**10, bytes_accessed=6 * 2**20, transcendentals=2 * 10**7),
    )(where, queries, *blocks)


def around(array, step):
    return lax.ppermute(array, "xc", [((n + 2 * step) % 8, n) for n in range(8)])


def across(array):
    return lax.ppermute(array, "yz", [(n ^ 1, n) for n in range(16)])


def swap(array):
    return lax.ppermute(array, "xc", [(n ^ 1, n) for n in range(8)])


def trade(array):
    return lax.all_to_all(array, "yz", split_axis=0, concat_axis=0, tiled=True, axis_index_groups=TRADERS)


def on_device(queries, keys, values):
    z, xc = lax.axis_index("yz") % 4, lax.axis_index("xc")
    kv = prepare(keys, values)
    own = lax.all_to_all(kv, "yz", split_axis=0, concat_axis=0, tiled=True)
    q = by_head(queries).reshape(8, CHUNK, HEAD_DIM)
    q, own = lax.optimization_barrier((q, own))
    own = own.reshape(4, 4, 2, TOK, HEAD_DIM)
    other = swap(own)
    q = trade(after(q, own)).reshape(4, PAIR, HEAD_DIM)
    inner = (z == 1) | (z == 2)
    half = around(jnp.where(inner, own[2:], own[:2]), 2)
    rest = across(half)
    far = jnp.concatenate([jnp.where(inner, rest, half), jnp.where(inner, half, rest)], axis=0)
    blocks, slots = [own, other], [xc, xc ^ 1]
    for step, block in ((1, around(own, 1)), (3, around(own, 3)), (2, far)):
        blocks += [block, swap(block)]
        slots += [(xc + 2 * step) % 8, (xc + 2 * step) % 8 ^ 1]
    where = jnp.stack([jnp.where(inner, 1, 0), xc] + slots).astype(jnp.int32)
    out = trade(attend(where, q, blocks))
    return out.transpose(1, 0, 2).reshape(queries.shape)


def solution(mesh):
    fine = Mesh(mesh.devices.reshape(tuple(SIZES.values())), tuple(SIZES))
    spec = P(tuple(SIZES), None)
    return jax.shard_map(
        on_device, mesh=fine, in_specs=(spec,) * 3, out_specs=spec, check_vma=False
    )
```

```python
import math

import jax
import jax.numpy as jnp
from jax import lax
from jax.experimental import pallas as pl
from jax.experimental.pallas import tpu as pltpu
from jax.sharding import Mesh, PartitionSpec as P

HEAD_DIM = 128
GROUP = 8
TOK = 64
SIZES = {"yz": 16, "xc": 8}
TRADERS = [[4 * y + z for y in range(4) for z in zs] for zs in ((0, 3), (1, 2))]
CHUNK = GROUP * TOK
PAIR = 2 * CHUNK
STEP = 256
SCALE_LOG2 = HEAD_DIM ** (-0.5) * math.log2(math.e)
LOW, HIGH = 2.0**-60, 2.0**100
HIDDEN = -1e30
VMEM = pl.BlockSpec(memory_space=pltpu.VMEM)


def prepare_kernel(k_ref, v_ref, kv_ref):
    i = lax.broadcasted_iota(jnp.int32, (HEAD_DIM, HEAD_DIM), 0)
    j = lax.broadcasted_iota(jnp.int32, (HEAD_DIM, HEAD_DIM), 1)
    parity = i & j
    for shift in (4, 2, 1):
        parity = parity ^ (parity >> shift)
    matrix = (1 - 2 * (parity & 1)).astype(jnp.float32).astype(jnp.bfloat16)
    heads = k_ref.shape[1] // HEAD_DIM
    for part, ref in enumerate((k_ref, v_ref)):
        rows = jnp.concatenate([ref[:, h * HEAD_DIM : (h + 1) * HEAD_DIM] for h in range(heads)], axis=0)
        turned = jnp.dot(rows, matrix, preferred_element_type=jnp.float32) * HEAD_DIM ** (-0.5)
        turned = turned.astype(jnp.bfloat16)
        for h in range(heads):
            for n in range(2):
                kv_ref[2 * h + n, part] = turned[h * TOK : (h + 1) * TOK]


def prepare(keys, values):
    return pl.pallas_call(
        prepare_kernel,
        out_shape=jax.ShapeDtypeStruct((16, 2, TOK, HEAD_DIM), jnp.bfloat16),
    )(keys, values)


def by_head_kernel(q_ref, o_ref):
    for h in range(o_ref.shape[0]):
        o_ref[h] = q_ref[:, h * HEAD_DIM : (h + 1) * HEAD_DIM]


def by_head(queries):
    heads = queries.shape[1] // HEAD_DIM
    return pl.pallas_call(
        by_head_kernel,
        out_shape=jax.ShapeDtypeStruct((heads, TOK, HEAD_DIM), jnp.bfloat16),
    )(queries)


def attend_kernel(*refs):
    where_ref, q_ref = refs[:2]
    block_refs = refs[2:10]
    o_ref, acc_pairs, bias, top, extremes = refs[10:]
    inner = where_ref[0]
    token = lax.broadcasted_iota(jnp.int32, (TOK, TOK), 0)
    key = lax.broadcasted_iota(jnp.int32, (TOK, TOK), 1)
    for b in range(8):
        ahead = where_ref[2 + b] - where_ref[1]
        bias[:, b * TOK : (b + 1) * TOK] = jnp.where(ahead * TOK + key <= token, 0.0, HIDDEN)

    def load(part, quads):
        def rows(y, z):
            turned = lax.rem(y + 2 * inner, 4)
            return [r[y if b < 6 else turned, z, part] for b, r in enumerate(block_refs)]

        return jnp.concatenate([piece for quad in quads for piece in rows(*quad)], axis=0)

    def scores(y, row, rows, quads, masked):
        x = (
            lax.dot_general(
                q_ref[y, pl.ds(row, rows), :],
                load(0, quads),
                (((1,), (1,)), ((), ())),
                preferred_element_type=jnp.float32,
            )
            * SCALE_LOG2
        )
        if masked:
            seen = x.shape[1] - bias.shape[1]
            hidden = x[:, seen:] + jnp.concatenate([bias[...]] * (rows // TOK), axis=0)
            x = jnp.concatenate([x[:, :seen], hidden], axis=1) if seen else hidden
        return x

    def weigh(weights, quads):
        values = load(1, quads)
        return jnp.dot(
            weights.astype(jnp.bfloat16),
            jnp.concatenate([values, jnp.ones_like(values)], axis=1),
            preferred_element_type=jnp.float32,
        )

    def run(y, jobs, fresh):
        acc = acc_pairs.at[y % 2]
        x = scores(y, jobs[0][0], STEP, *jobs[0][1:])
        for n, (row, quads, _) in enumerate(jobs):
            weights = jnp.exp2(x)
            if n + 1 < len(jobs):
                x = scores(y, jobs[n + 1][0], STEP, *jobs[n + 1][1:])
            out = weigh(weights, quads)
            at = pl.ds(row, STEP)
            acc[at, :] = out if fresh else acc[at, :] + out

    def same_y(y, zs):
        jobs = [
            (row, [(y, z) for z in range(zs[row // CHUNK] + 1)], True) for row in range(0, PAIR, STEP)
        ]
        finish(jnp.maximum(y, 1) - 1)
        run(y, jobs, True)

    def store(y, m, acc):
        rows = slice(m * CHUNK, (m + 1) * CHUNK)
        out = (acc[rows, :HEAD_DIM] / acc[rows, HEAD_DIM:]).astype(jnp.bfloat16)
        for h in range(GROUP):
            o_ref[2 * y + m, :, h * HEAD_DIM : (h + 1) * HEAD_DIM] = out[h * TOK : (h + 1) * TOK]

    def finish(y):
        acc = acc_pairs.at[y % 2]
        for m in range(2):
            store(y, m, acc)
        total = acc[:, HEAD_DIM:].reshape(PAIR // 8, 8, HEAD_DIM)
        extremes[0] = jnp.minimum(extremes[0], jnp.min(total, axis=0))
        extremes[1] = jnp.maximum(extremes[1], jnp.max(total, axis=0))

    def pair(y, carry):
        pl.when(inner == 0)(lambda: same_y(y, (0, 3)))
        pl.when(inner == 1)(lambda: same_y(y, (1, 2)))

        def earlier(key_y, carry):
            quads = [(key_y, z) for z in range(4)]
            run(y, [(row, quads, False) for row in range(0, PAIR, STEP)], False)
            return carry

        lax.fori_loop(0, y, earlier, 0)
        return carry

    acc_pairs[0] = jnp.ones((PAIR, 2 * HEAD_DIM), jnp.float32)
    extremes[...] = jnp.ones((2, 8, HEAD_DIM), jnp.float32)
    lax.fori_loop(0, 4, pair, 0)
    finish(3)
    fine = (extremes[0] >= LOW) & (extremes[1] <= HIGH)
    bad = jnp.max(jnp.where(fine, 0.0, 1.0))

    @pl.when(bad > 0.0)
    def _():
        acc = acc_pairs.at[0]

        def exact(y, m, quad, first):
            row = pl.multiple_of(m * CHUNK, CHUNK)
            rows = pl.ds(row, CHUNK)
            x = scores(y, row, CHUNK, [quad], first)
            high = jnp.max(x, axis=1, keepdims=True)
            if first:
                acc[rows, :] = weigh(jnp.exp2(x - high), [quad])
            else:
                before = top[:, :1]
                high = jnp.maximum(high, before)
                acc[rows, :] = acc[rows, :] * jnp.exp2(before - high) + weigh(jnp.exp2(x - high), [quad])
            top[...] = jnp.broadcast_to(high, top.shape)

        def exact_chunk(n, m):
            z = inner + m * (3 - 2 * inner)
            exact(n, m, (n, z), True)

            def others(k, carry):
                exact(n, m, (k // 4, k % 4), False)
                return carry

            lax.fori_loop(0, 4 * n + z, others, 0)
            store(n, m, acc)

        def exact_pair(y, carry):
            for m in range(2):
                exact_chunk(y, m)
            return carry

        lax.fori_loop(0, 4, exact_pair, 0)


def attend(where, queries, blocks):
    return pl.pallas_call(
        attend_kernel,
        out_shape=jax.ShapeDtypeStruct((8, TOK, GROUP * HEAD_DIM), jnp.bfloat16),
        in_specs=[pl.BlockSpec(memory_space=pltpu.SMEM)] + [VMEM] * 9,
        out_specs=VMEM,
        scratch_shapes=[
            pltpu.VMEM((2, PAIR, 2 * HEAD_DIM), jnp.float32),
            pltpu.VMEM((TOK, 8 * TOK), jnp.float32),
            pltpu.VMEM((CHUNK, HEAD_DIM), jnp.float32),
            pltpu.VMEM((2, 8, HEAD_DIM), jnp.float32),
        ],
        compiler_params=pltpu.CompilerParams(vmem_limit_bytes=20 * 2**20),
        cost_estimate=pl.CostEstimate(flops=2 * 10**10, bytes_accessed=6 * 2**20, transcendentals=2 * 10**7),
    )(where, queries, *blocks)


def around(array, step):
    return lax.ppermute(array, "xc", [((n + 2 * step) % 8, n) for n in range(8)])


def across(array):
    return lax.ppermute(array, "yz", [(n ^ 1, n) for n in range(16)])


def swap(array):
    return lax.ppermute(array, "xc", [(n ^ 1, n) for n in range(8)])


def trade(array):
    return lax.all_to_all(array, "yz", split_axis=0, concat_axis=0, tiled=True, axis_index_groups=TRADERS)


def on_device(queries, keys, values):
    z, xc = lax.axis_index("yz") % 4, lax.axis_index("xc")
    kv = prepare(keys, values)
    own = lax.all_to_all(kv, "yz", split_axis=0, concat_axis=0, tiled=True)
    q = by_head(queries).reshape(8, CHUNK, HEAD_DIM)
    q, own = lax.optimization_barrier((q, own))
    own = own.reshape(4, 4, 2, TOK, HEAD_DIM)
    other = swap(own)
    q = trade(q).reshape(4, PAIR, HEAD_DIM)
    inner = (z == 1) | (z == 2)
    half = around(jnp.where(inner, own[2:], own[:2]), 2)
    rest = across(half)
    far = jnp.concatenate([half, rest])
    far_other = swap(far)
    blocks, slots = [own, other], [xc, xc ^ 1]
    for step, block in ((1, around(own, 1)), (3, around(own, 3)), (2, far)):
        blocks += [block, far_other if step == 2 else swap(block)]
        slots += [(xc + 2 * step) % 8, (xc + 2 * step) % 8 ^ 1]
    where = jnp.stack([jnp.where(inner, 1, 0), xc] + slots).astype(jnp.int32)
    out = trade(attend(where, q, blocks))
    return out.transpose(1, 0, 2).reshape(queries.shape)


def solution(mesh):
    fine = Mesh(mesh.devices.reshape(tuple(SIZES.values())), tuple(SIZES))
    spec = P(tuple(SIZES), None)
    return jax.shard_map(
        on_device, mesh=fine, in_specs=(spec,) * 3, out_specs=spec, check_vma=False
    )
```

```python
import math

import jax
import jax.numpy as jnp
from jax import lax
from jax.experimental import pallas as pl
from jax.experimental.pallas import tpu as pltpu
from jax.sharding import Mesh, PartitionSpec as P

HEAD_DIM = 128
GROUP = 8
TOK = 64
SIZES = {"yz": 16, "xc": 8}
TRADERS = [[4 * y + z for y in range(4) for z in zs] for zs in ((0, 3), (1, 2))]
CHUNK = GROUP * TOK
PAIR = 2 * CHUNK
STEP = 256
SCALE_LOG2 = HEAD_DIM ** (-0.5) * math.log2(math.e)
LOW, HIGH = 2.0**-60, 2.0**100
HIDDEN = -1e30
VMEM = pl.BlockSpec(memory_space=pltpu.VMEM)


def prepare_kernel(k_ref, v_ref, kv_ref):
    i = lax.broadcasted_iota(jnp.int32, (HEAD_DIM, HEAD_DIM), 0)
    j = lax.broadcasted_iota(jnp.int32, (HEAD_DIM, HEAD_DIM), 1)
    parity = i & j
    for shift in (4, 2, 1):
        parity = parity ^ (parity >> shift)
    matrix = (1 - 2 * (parity & 1)).astype(jnp.float32).astype(jnp.bfloat16)
    heads = k_ref.shape[1] // HEAD_DIM
    for part, ref in enumerate((k_ref, v_ref)):
        rows = jnp.concatenate([ref[:, h * HEAD_DIM : (h + 1) * HEAD_DIM] for h in range(heads)], axis=0)
        turned = jnp.dot(rows, matrix, preferred_element_type=jnp.float32) * HEAD_DIM ** (-0.5)
        turned = turned.astype(jnp.bfloat16)
        for h in range(heads):
            for n in range(2):
                kv_ref[2 * h + n, part] = turned[h * TOK : (h + 1) * TOK]


def prepare(keys, values):
    return pl.pallas_call(
        prepare_kernel,
        out_shape=jax.ShapeDtypeStruct((16, 2, TOK, HEAD_DIM), jnp.bfloat16),
    )(keys, values)


def by_head_kernel(q_ref, o_ref):
    for h in range(o_ref.shape[0]):
        o_ref[h] = q_ref[:, h * HEAD_DIM : (h + 1) * HEAD_DIM]


def by_head(queries):
    heads = queries.shape[1] // HEAD_DIM
    return pl.pallas_call(
        by_head_kernel,
        out_shape=jax.ShapeDtypeStruct((heads, TOK, HEAD_DIM), jnp.bfloat16),
    )(queries)


def after_kernel(array_ref, token_ref, o_ref):
    del array_ref, token_ref, o_ref


def after(array, token):
    return pl.pallas_call(
        after_kernel,
        out_shape=jax.ShapeDtypeStruct(array.shape, array.dtype),
        in_specs=[pl.BlockSpec(memory_space=pl.ANY)] * 2,
        out_specs=pl.BlockSpec(memory_space=pl.ANY),
        input_output_aliases={0: 0},
        cost_estimate=pl.CostEstimate(flops=5 * 10**9, bytes_accessed=0, transcendentals=0),
    )(array, token)


def attend_kernel(*refs):
    where_ref, q_ref = refs[:2]
    block_refs = refs[2:10]
    o_ref, acc_pairs, bias, top, extremes = refs[10:]
    inner = where_ref[0]
    token = lax.broadcasted_iota(jnp.int32, (TOK, TOK), 0)
    key = lax.broadcasted_iota(jnp.int32, (TOK, TOK), 1)
    for b in range(8):
        ahead = where_ref[2 + b] - where_ref[1]
        bias[:, b * TOK : (b + 1) * TOK] = jnp.where(ahead * TOK + key <= token, 0.0, HIDDEN)

    def load(part, quads):
        return jnp.concatenate([r[(*quad, part)] for quad in quads for r in block_refs], axis=0)

    def scores(y, row, rows, quads, masked):
        x = (
            lax.dot_general(
                q_ref[y, pl.ds(row, rows), :],
                load(0, quads),
                (((1,), (1,)), ((), ())),
                preferred_element_type=jnp.float32,
            )
            * SCALE_LOG2
        )
        if masked:
            seen = x.shape[1] - bias.shape[1]
            hidden = x[:, seen:] + jnp.concatenate([bias[...]] * (rows // TOK), axis=0)
            x = jnp.concatenate([x[:, :seen], hidden], axis=1) if seen else hidden
        return x

    def weigh(weights, quads):
        values = load(1, quads)
        return jnp.dot(
            weights.astype(jnp.bfloat16),
            jnp.concatenate([values, jnp.ones_like(values)], axis=1),
            preferred_element_type=jnp.float32,
        )

    def run(y, jobs, fresh):
        acc = acc_pairs.at[y % 2]
        x = scores(y, jobs[0][0], STEP, *jobs[0][1:])
        for n, (row, quads, _) in enumerate(jobs):
            weights = jnp.exp2(x)
            if n + 1 < len(jobs):
                x = scores(y, jobs[n + 1][0], STEP, *jobs[n + 1][1:])
            out = weigh(weights, quads)
            at = pl.ds(row, STEP)
            acc[at, :] = out if fresh else acc[at, :] + out

    def same_y(y, zs):
        jobs = [
            (row, [(y, z) for z in range(zs[row // CHUNK] + 1)], True) for row in range(0, PAIR, STEP)
        ]
        finish(jnp.maximum(y, 1) - 1)
        run(y, jobs, True)

    def store(y, m, acc):
        rows = slice(m * CHUNK, (m + 1) * CHUNK)
        out = (acc[rows, :HEAD_DIM] / acc[rows, HEAD_DIM:]).astype(jnp.bfloat16)
        for h in range(GROUP):
            o_ref[2 * y + m, :, h * HEAD_DIM : (h + 1) * HEAD_DIM] = out[h * TOK : (h + 1) * TOK]

    def finish(y):
        acc = acc_pairs.at[y % 2]
        for m in range(2):
            store(y, m, acc)
        total = acc[:, HEAD_DIM:].reshape(PAIR // 8, 8, HEAD_DIM)
        extremes[0] = jnp.minimum(extremes[0], jnp.min(total, axis=0))
        extremes[1] = jnp.maximum(extremes[1], jnp.max(total, axis=0))

    def pair(y, carry):
        pl.when(inner == 0)(lambda: same_y(y, (0, 3)))
        pl.when(inner == 1)(lambda: same_y(y, (1, 2)))

        def earlier(key_y, carry):
            quads = [(key_y, z) for z in range(4)]
            run(y, [(row, quads, False) for row in range(0, PAIR, STEP)], False)
            return carry

        lax.fori_loop(0, y, earlier, 0)
        return carry

    acc_pairs[0] = jnp.ones((PAIR, 2 * HEAD_DIM), jnp.float32)
    extremes[...] = jnp.ones((2, 8, HEAD_DIM), jnp.float32)
    lax.fori_loop(0, 4, pair, 0)
    finish(3)
    fine = (extremes[0] >= LOW) & (extremes[1] <= HIGH)
    bad = jnp.max(jnp.where(fine, 0.0, 1.0))

    @pl.when(bad > 0.0)
    def _():
        acc = acc_pairs.at[0]

        def exact(y, m, quad, first):
            row = pl.multiple_of(m * CHUNK, CHUNK)
            rows = pl.ds(row, CHUNK)
            x = scores(y, row, CHUNK, [quad], first)
            high = jnp.max(x, axis=1, keepdims=True)
            if first:
                acc[rows, :] = weigh(jnp.exp2(x - high), [quad])
            else:
                before = top[:, :1]
                high = jnp.maximum(high, before)
                acc[rows, :] = acc[rows, :] * jnp.exp2(before - high) + weigh(jnp.exp2(x - high), [quad])
            top[...] = jnp.broadcast_to(high, top.shape)

        def exact_chunk(n, m):
            z = inner + m * (3 - 2 * inner)
            exact(n, m, (n, z), True)

            def others(k, carry):
                exact(n, m, (k // 4, k % 4), False)
                return carry

            lax.fori_loop(0, 4 * n + z, others, 0)
            store(n, m, acc)

        def exact_pair(y, carry):
            for m in range(2):
                exact_chunk(y, m)
            return carry

        lax.fori_loop(0, 4, exact_pair, 0)


def attend(where, queries, blocks):
    return pl.pallas_call(
        attend_kernel,
        out_shape=jax.ShapeDtypeStruct((8, TOK, GROUP * HEAD_DIM), jnp.bfloat16),
        in_specs=[pl.BlockSpec(memory_space=pltpu.SMEM)] + [VMEM] * 9,
        out_specs=VMEM,
        scratch_shapes=[
            pltpu.VMEM((2, PAIR, 2 * HEAD_DIM), jnp.float32),
            pltpu.VMEM((TOK, 8 * TOK), jnp.float32),
            pltpu.VMEM((CHUNK, HEAD_DIM), jnp.float32),
            pltpu.VMEM((2, 8, HEAD_DIM), jnp.float32),
        ],
        compiler_params=pltpu.CompilerParams(vmem_limit_bytes=20 * 2**20),
        cost_estimate=pl.CostEstimate(flops=2 * 10**10, bytes_accessed=6 * 2**20, transcendentals=2 * 10**7),
    )(where, queries, *blocks)


def around(array, step):
    return lax.ppermute(array, "xc", [((n + 2 * step) % 8, n) for n in range(8)])


def across(array):
    return lax.ppermute(array, "yz", [(n ^ 1, n) for n in range(16)])


def swap(array):
    return lax.ppermute(array, "xc", [(n ^ 1, n) for n in range(8)])


def trade(array):
    return lax.all_to_all(array, "yz", split_axis=0, concat_axis=0, tiled=True, axis_index_groups=TRADERS)


def on_device(queries, keys, values):
    z, xc = lax.axis_index("yz") % 4, lax.axis_index("xc")
    kv = prepare(keys, values)
    own = lax.all_to_all(kv, "yz", split_axis=0, concat_axis=0, tiled=True)
    q = by_head(queries).reshape(8, CHUNK, HEAD_DIM)
    q, own = lax.optimization_barrier((q, own))
    own = own.reshape(4, 4, 2, TOK, HEAD_DIM)
    other = swap(own)
    q = trade(after(q, own[0, 0, 0, :16])).reshape(4, PAIR, HEAD_DIM)
    inner = (z == 1) | (z == 2)
    half = around(jnp.where(inner, own[2:], own[:2]), 2)
    rest = across(half)
    far = jnp.concatenate([jnp.where(inner, rest, half), jnp.where(inner, half, rest)], axis=0)
    blocks, slots = [own, other], [xc, xc ^ 1]
    for step, block in ((1, around(own, 1)), (3, around(own, 3)), (2, far)):
        blocks += [block, swap(block)]
        slots += [(xc + 2 * step) % 8, (xc + 2 * step) % 8 ^ 1]
    where = jnp.stack([jnp.where(inner, 1, 0), xc] + slots).astype(jnp.int32)
    out = trade(attend(where, q, blocks))
    return out.transpose(1, 0, 2).reshape(queries.shape)


def solution(mesh):
    fine = Mesh(mesh.devices.reshape(tuple(SIZES.values())), tuple(SIZES))
    spec = P(tuple(SIZES), None)
    return jax.shard_map(
        on_device, mesh=fine, in_specs=(spec,) * 3, out_specs=spec, check_vma=False
    )
```

```python
import math

import jax
import jax.numpy as jnp
from jax import lax
from jax.experimental import pallas as pl
from jax.experimental.pallas import tpu as pltpu
from jax.sharding import Mesh, PartitionSpec as P

HEAD_DIM = 128
GROUP = 8
TOK = 64
SIZES = {"yz": 16, "xc": 8}
TRADERS = [[4 * y + z for y in range(4) for z in zs] for zs in ((0, 3), (1, 2))]
CHUNK = GROUP * TOK
PAIR = 2 * CHUNK
STEP = 256
SCALE_LOG2 = HEAD_DIM ** (-0.5) * math.log2(math.e)
LOW, HIGH = 2.0**-60, 2.0**100
HIDDEN = -1e30
VMEM = pl.BlockSpec(memory_space=pltpu.VMEM)


def prepare_kernel(k_ref, v_ref, kv_ref):
    i = lax.broadcasted_iota(jnp.int32, (HEAD_DIM, HEAD_DIM), 0)
    j = lax.broadcasted_iota(jnp.int32, (HEAD_DIM, HEAD_DIM), 1)
    parity = i & j
    for shift in (4, 2, 1):
        parity = parity ^ (parity >> shift)
    matrix = (1 - 2 * (parity & 1)).astype(jnp.float32).astype(jnp.bfloat16)
    heads = k_ref.shape[1] // HEAD_DIM
    for part, ref in enumerate((k_ref, v_ref)):
        rows = jnp.concatenate([ref[:, h * HEAD_DIM : (h + 1) * HEAD_DIM] for h in range(heads)], axis=0)
        turned = jnp.dot(rows, matrix, preferred_element_type=jnp.float32) * HEAD_DIM ** (-0.5)
        turned = turned.astype(jnp.bfloat16)
        for h in range(heads):
            for n in range(2):
                kv_ref[2 * h + n, part] = turned[h * TOK : (h + 1) * TOK]


def prepare(keys, values):
    return pl.pallas_call(
        prepare_kernel,
        out_shape=jax.ShapeDtypeStruct((16, 2, TOK, HEAD_DIM), jnp.bfloat16),
    )(keys, values)


def by_head_kernel(q_ref, o_ref):
    for h in range(o_ref.shape[0]):
        o_ref[h] = q_ref[:, h * HEAD_DIM : (h + 1) * HEAD_DIM]


def by_head(queries):
    heads = queries.shape[1] // HEAD_DIM
    return pl.pallas_call(
        by_head_kernel,
        out_shape=jax.ShapeDtypeStruct((heads, TOK, HEAD_DIM), jnp.bfloat16),
    )(queries)


def attend_kernel(*refs):
    where_ref, q_ref = refs[:2]
    block_refs = refs[2:10]
    o_ref, acc_pairs, bias, top, extremes = refs[10:]
    inner = where_ref[0]
    token = lax.broadcasted_iota(jnp.int32, (TOK, TOK), 0)
    key = lax.broadcasted_iota(jnp.int32, (TOK, TOK), 1)
    for b in range(8):
        ahead = where_ref[2 + b] - where_ref[1]
        bias[:, b * TOK : (b + 1) * TOK] = jnp.where(ahead * TOK + key <= token, 0.0, HIDDEN)

    def load(part, quads):
        def rows(y, z):
            turned = lax.rem(y + 2 * inner, 4)
            return [r[y if b < 6 else turned, z, part] for b, r in enumerate(block_refs)]

        return jnp.concatenate([piece for quad in quads for piece in rows(*quad)], axis=0)

    def scores(y, row, rows, quads, masked):
        x = (
            lax.dot_general(
                q_ref[y, pl.ds(row, rows), :],
                load(0, quads),
                (((1,), (1,)), ((), ())),
                preferred_element_type=jnp.float32,
            )
            * SCALE_LOG2
        )
        if masked:
            seen = x.shape[1] - bias.shape[1]
            hidden = x[:, seen:] + jnp.concatenate([bias[...]] * (rows // TOK), axis=0)
            x = jnp.concatenate([x[:, :seen], hidden], axis=1) if seen else hidden
        return x

    def weigh(weights, quads):
        values = load(1, quads)
        return jnp.dot(
            weights.astype(jnp.bfloat16),
            jnp.concatenate([values, jnp.ones_like(values)], axis=1),
            preferred_element_type=jnp.float32,
        )

    def run(y, jobs, fresh):
        acc = acc_pairs.at[y % 2]
        x = scores(y, jobs[0][0], STEP, *jobs[0][1:])
        for n, (row, quads, _) in enumerate(jobs):
            weights = jnp.exp2(x)
            if n + 1 < len(jobs):
                x = scores(y, jobs[n + 1][0], STEP, *jobs[n + 1][1:])
            out = weigh(weights, quads)
            at = pl.ds(row, STEP)
            acc[at, :] = out if fresh else acc[at, :] + out

    def same_y(y, zs):
        jobs = [
            (row, [(y, z) for z in range(zs[row // CHUNK] + 1)], True) for row in range(0, PAIR, STEP)
        ]
        finish(jnp.maximum(y, 1) - 1)
        run(y, jobs, True)

    def store(y, m, acc):
        rows = slice(m * CHUNK, (m + 1) * CHUNK)
        out = (acc[rows, :HEAD_DIM] / acc[rows, HEAD_DIM:]).astype(jnp.bfloat16)
        for h in range(GROUP):
            o_ref[2 * y + m, :, h * HEAD_DIM : (h + 1) * HEAD_DIM] = out[h * TOK : (h + 1) * TOK]

    def finish(y):
        acc = acc_pairs.at[y % 2]
        for m in range(2):
            store(y, m, acc)
        total = acc[:, HEAD_DIM:].reshape(PAIR // 8, 8, HEAD_DIM)
        extremes[0] = jnp.minimum(extremes[0], jnp.min(total, axis=0))
        extremes[1] = jnp.maximum(extremes[1], jnp.max(total, axis=0))

    def pair(y, carry):
        pl.when(inner == 0)(lambda: same_y(y, (0, 3)))
        pl.when(inner == 1)(lambda: same_y(y, (1, 2)))

        def earlier(key_y, carry):
            quads = [(key_y, z) for z in range(4)]
            run(y, [(row, quads, False) for row in range(0, PAIR, STEP)], False)
            return carry

        lax.fori_loop(0, y, earlier, 0)
        return carry

    acc_pairs[0] = jnp.ones((PAIR, 2 * HEAD_DIM), jnp.float32)
    extremes[...] = jnp.ones((2, 8, HEAD_DIM), jnp.float32)
    lax.fori_loop(0, 4, pair, 0)
    finish(3)
    fine = (extremes[0] >= LOW) & (extremes[1] <= HIGH)
    bad = jnp.max(jnp.where(fine, 0.0, 1.0))

    @pl.when(bad > 0.0)
    def _():
        acc = acc_pairs.at[0]

        def exact(y, m, quad, first):
            row = pl.multiple_of(m * CHUNK, CHUNK)
            rows = pl.ds(row, CHUNK)
            x = scores(y, row, CHUNK, [quad], first)
            high = jnp.max(x, axis=1, keepdims=True)
            if first:
                acc[rows, :] = weigh(jnp.exp2(x - high), [quad])
            else:
                before = top[:, :1]
                high = jnp.maximum(high, before)
                acc[rows, :] = acc[rows, :] * jnp.exp2(before - high) + weigh(jnp.exp2(x - high), [quad])
            top[...] = jnp.broadcast_to(high, top.shape)

        def exact_chunk(n, m):
            z = inner + m * (3 - 2 * inner)
            exact(n, m, (n, z), True)

            def others(k, carry):
                exact(n, m, (k // 4, k % 4), False)
                return carry

            lax.fori_loop(0, 4 * n + z, others, 0)
            store(n, m, acc)

        def exact_pair(y, carry):
            for m in range(2):
                exact_chunk(y, m)
            return carry

        lax.fori_loop(0, 4, exact_pair, 0)


def attend(where, queries, blocks):
    return pl.pallas_call(
        attend_kernel,
        out_shape=jax.ShapeDtypeStruct((8, TOK, GROUP * HEAD_DIM), jnp.bfloat16),
        in_specs=[pl.BlockSpec(memory_space=pltpu.SMEM)] + [VMEM] * 9,
        out_specs=VMEM,
        scratch_shapes=[
            pltpu.VMEM((2, PAIR, 2 * HEAD_DIM), jnp.float32),
            pltpu.VMEM((TOK, 8 * TOK), jnp.float32),
            pltpu.VMEM((CHUNK, HEAD_DIM), jnp.float32),
            pltpu.VMEM((2, 8, HEAD_DIM), jnp.float32),
        ],
        compiler_params=pltpu.CompilerParams(vmem_limit_bytes=20 * 2**20),
        cost_estimate=pl.CostEstimate(flops=2 * 10**10, bytes_accessed=6 * 2**20, transcendentals=2 * 10**7),
    )(where, queries, *blocks)


def around(array, step):
    return lax.ppermute(array, "xc", [((n + 2 * step) % 8, n) for n in range(8)])


def across(array):
    return lax.ppermute(array, "yz", [(n ^ 1, n) for n in range(16)])


def swap(array):
    return lax.ppermute(array, "xc", [(n ^ 1, n) for n in range(8)])


def trade(array):
    return lax.all_to_all(array, "yz", split_axis=0, concat_axis=0, tiled=True, axis_index_groups=TRADERS)


def on_device(queries, keys, values):
    z, xc = lax.axis_index("yz") % 4, lax.axis_index("xc")
    kv = prepare(keys, values)
    own = lax.all_to_all(kv, "yz", split_axis=0, concat_axis=0, tiled=True)
    q = by_head(queries).reshape(8, CHUNK, HEAD_DIM)
    q, own = lax.optimization_barrier((q, own))
    own = own.reshape(4, 4, 2, TOK, HEAD_DIM)
    other = swap(own)
    q = trade(q).reshape(4, PAIR, HEAD_DIM)
    inner = (z == 1) | (z == 2)
    half = around(jnp.where(inner, own[2:], own[:2]), 2)
    rest = across(half)
    near = [around(own, step) for step in (1, 3)]
    near[0], near[1], rest = lax.optimization_barrier((near[0], near[1], rest))
    blocks, slots = [own, other], [xc, xc ^ 1]
    for step, block in ((1, near[0]), (3, near[1]), (2, jnp.concatenate([half, rest]))):
        blocks += [block, swap(block)]
        slots += [(xc + 2 * step) % 8, (xc + 2 * step) % 8 ^ 1]
    where = jnp.stack([jnp.where(inner, 1, 0), xc] + slots).astype(jnp.int32)
    out = trade(attend(where, q, blocks))
    return out.transpose(1, 0, 2).reshape(queries.shape)


def solution(mesh):
    fine = Mesh(mesh.devices.reshape(tuple(SIZES.values())), tuple(SIZES))
    spec = P(tuple(SIZES), None)
    return jax.shard_map(
        on_device, mesh=fine, in_specs=(spec,) * 3, out_specs=spec, check_vma=False
    )
```

```python
import math

import jax
import jax.numpy as jnp
from jax import lax
from jax.experimental import pallas as pl
from jax.experimental.pallas import tpu as pltpu
from jax.sharding import Mesh, PartitionSpec as P

HEAD_DIM = 128
GROUP = 8
TOK = 64
SIZES = {"yz": 16, "xc": 8}
TRADERS = [[4 * y + z for y in range(4) for z in zs] for zs in ((0, 3), (1, 2))]
CHUNK = GROUP * TOK
PAIR = 2 * CHUNK
STEP = 256
SCALE_LOG2 = HEAD_DIM ** (-0.5) * math.log2(math.e)
LOW, HIGH = 2.0**-60, 2.0**100
HIDDEN = -1e30
VMEM = pl.BlockSpec(memory_space=pltpu.VMEM)


def prepare_kernel(k_ref, v_ref, kv_ref):
    i = lax.broadcasted_iota(jnp.int32, (HEAD_DIM, HEAD_DIM), 0)
    j = lax.broadcasted_iota(jnp.int32, (HEAD_DIM, HEAD_DIM), 1)
    parity = i & j
    for shift in (4, 2, 1):
        parity = parity ^ (parity >> shift)
    matrix = (1 - 2 * (parity & 1)).astype(jnp.float32).astype(jnp.bfloat16)
    heads = k_ref.shape[1] // HEAD_DIM
    for part, ref in enumerate((k_ref, v_ref)):
        rows = jnp.concatenate([ref[:, h * HEAD_DIM : (h + 1) * HEAD_DIM] for h in range(heads)], axis=0)
        turned = jnp.dot(rows, matrix, preferred_element_type=jnp.float32) * HEAD_DIM ** (-0.5)
        turned = turned.astype(jnp.bfloat16)
        for h in range(heads):
            for n in range(2):
                kv_ref[2 * h + n, part] = turned[h * TOK : (h + 1) * TOK]


def prepare(keys, values):
    return pl.pallas_call(
        prepare_kernel,
        out_shape=jax.ShapeDtypeStruct((16, 2, TOK, HEAD_DIM), jnp.bfloat16),
    )(keys, values)


def by_head_kernel(q_ref, o_ref):
    for h in range(o_ref.shape[0]):
        o_ref[h] = q_ref[:, h * HEAD_DIM : (h + 1) * HEAD_DIM]


def by_head(queries):
    heads = queries.shape[1] // HEAD_DIM
    return pl.pallas_call(
        by_head_kernel,
        out_shape=jax.ShapeDtypeStruct((heads, TOK, HEAD_DIM), jnp.bfloat16),
    )(queries)


def after_kernel(array_ref, token_ref, o_ref):
    del array_ref, token_ref, o_ref


def after(array, token):
    return pl.pallas_call(
        after_kernel,
        out_shape=jax.ShapeDtypeStruct(array.shape, array.dtype),
        in_specs=[pl.BlockSpec(memory_space=pl.ANY)] * 2,
        out_specs=pl.BlockSpec(memory_space=pl.ANY),
        input_output_aliases={0: 0},
        cost_estimate=pl.CostEstimate(flops=5 * 10**9, bytes_accessed=0, transcendentals=0),
    )(array, token)


def attend_kernel(*refs):
    where_ref, q_ref = refs[:2]
    block_refs = refs[2:10]
    o_ref, acc_pairs, bias, top, extremes = refs[10:]
    inner = where_ref[0]
    token = lax.broadcasted_iota(jnp.int32, (TOK, TOK), 0)
    key = lax.broadcasted_iota(jnp.int32, (TOK, TOK), 1)
    for b in range(8):
        ahead = where_ref[2 + b] - where_ref[1]
        bias[:, b * TOK : (b + 1) * TOK] = jnp.where(ahead * TOK + key <= token, 0.0, HIDDEN)

    def load(part, quads):
        return jnp.concatenate([r[(*quad, part)] for quad in quads for r in block_refs], axis=0)

    def scores(y, row, rows, quads, masked):
        x = (
            lax.dot_general(
                q_ref[y, pl.ds(row, rows), :],
                load(0, quads),
                (((1,), (1,)), ((), ())),
                preferred_element_type=jnp.float32,
            )
            * SCALE_LOG2
        )
        if masked:
            seen = x.shape[1] - bias.shape[1]
            hidden = x[:, seen:] + jnp.concatenate([bias[...]] * (rows // TOK), axis=0)
            x = jnp.concatenate([x[:, :seen], hidden], axis=1) if seen else hidden
        return x

    def weigh(weights, quads):
        values = load(1, quads)
        return jnp.dot(
            weights.astype(jnp.bfloat16),
            jnp.concatenate([values, jnp.ones_like(values)], axis=1),
            preferred_element_type=jnp.float32,
        )

    def run(y, jobs, fresh):
        acc = acc_pairs.at[y % 2]
        x = scores(y, jobs[0][0], STEP, *jobs[0][1:])
        for n, (row, quads, _) in enumerate(jobs):
            weights = jnp.exp2(x)
            if n + 1 < len(jobs):
                x = scores(y, jobs[n + 1][0], STEP, *jobs[n + 1][1:])
            out = weigh(weights, quads)
            at = pl.ds(row, STEP)
            acc[at, :] = out if fresh else acc[at, :] + out

    def same_y(y, zs):
        jobs = [
            (row, [(y, z) for z in range(zs[row // CHUNK] + 1)], True) for row in range(0, PAIR, STEP)
        ]
        finish(jnp.maximum(y, 1) - 1)
        run(y, jobs, True)

    def store(y, m, acc):
        rows = slice(m * CHUNK, (m + 1) * CHUNK)
        out = (acc[rows, :HEAD_DIM] / acc[rows, HEAD_DIM:]).astype(jnp.bfloat16)
        for h in range(GROUP):
            o_ref[2 * y + m, :, h * HEAD_DIM : (h + 1) * HEAD_DIM] = out[h * TOK : (h + 1) * TOK]

    def finish(y):
        acc = acc_pairs.at[y % 2]
        for m in range(2):
            store(y, m, acc)
        total = acc[:, HEAD_DIM:].reshape(PAIR // 8, 8, HEAD_DIM)
        extremes[0] = jnp.minimum(extremes[0], jnp.min(total, axis=0))
        extremes[1] = jnp.maximum(extremes[1], jnp.max(total, axis=0))

    def pair(y, carry):
        pl.when(inner == 0)(lambda: same_y(y, (0, 3)))
        pl.when(inner == 1)(lambda: same_y(y, (1, 2)))

        def earlier(key_y, carry):
            quads = [(key_y, z) for z in range(4)]
            run(y, [(row, quads, False) for row in range(0, PAIR, STEP)], False)
            return carry

        lax.fori_loop(0, y, earlier, 0)
        return carry

    acc_pairs[0] = jnp.ones((PAIR, 2 * HEAD_DIM), jnp.float32)
    extremes[...] = jnp.ones((2, 8, HEAD_DIM), jnp.float32)
    lax.fori_loop(0, 4, pair, 0)
    finish(3)
    fine = (extremes[0] >= LOW) & (extremes[1] <= HIGH)
    bad = jnp.max(jnp.where(fine, 0.0, 1.0))

    @pl.when(bad > 0.0)
    def _():
        acc = acc_pairs.at[0]

        def exact(y, m, quad, first):
            row = pl.multiple_of(m * CHUNK, CHUNK)
            rows = pl.ds(row, CHUNK)
            x = scores(y, row, CHUNK, [quad], first)
            high = jnp.max(x, axis=1, keepdims=True)
            if first:
                acc[rows, :] = weigh(jnp.exp2(x - high), [quad])
            else:
                before = top[:, :1]
                high = jnp.maximum(high, before)
                acc[rows, :] = acc[rows, :] * jnp.exp2(before - high) + weigh(jnp.exp2(x - high), [quad])
            top[...] = jnp.broadcast_to(high, top.shape)

        def exact_chunk(n, m):
            z = inner + m * (3 - 2 * inner)
            exact(n, m, (n, z), True)

            def others(k, carry):
                exact(n, m, (k // 4, k % 4), False)
                return carry

            lax.fori_loop(0, 4 * n + z, others, 0)
            store(n, m, acc)

        def exact_pair(y, carry):
            for m in range(2):
                exact_chunk(y, m)
            return carry

        lax.fori_loop(0, 4, exact_pair, 0)


def attend(where, queries, blocks):
    return pl.pallas_call(
        attend_kernel,
        out_shape=jax.ShapeDtypeStruct((8, TOK, GROUP * HEAD_DIM), jnp.bfloat16),
        in_specs=[pl.BlockSpec(memory_space=pltpu.SMEM)] + [VMEM] * 9,
        out_specs=VMEM,
        scratch_shapes=[
            pltpu.VMEM((2, PAIR, 2 * HEAD_DIM), jnp.float32),
            pltpu.VMEM((TOK, 8 * TOK), jnp.float32),
            pltpu.VMEM((CHUNK, HEAD_DIM), jnp.float32),
            pltpu.VMEM((2, 8, HEAD_DIM), jnp.float32),
        ],
        compiler_params=pltpu.CompilerParams(vmem_limit_bytes=20 * 2**20),
        cost_estimate=pl.CostEstimate(flops=2 * 10**10, bytes_accessed=6 * 2**20, transcendentals=2 * 10**7),
    )(where, queries, *blocks)


def around(array, step):
    return lax.ppermute(array, "xc", [((n + 2 * step) % 8, n) for n in range(8)])


def across(array):
    return lax.ppermute(array, "yz", [(n ^ 1, n) for n in range(16)])


def swap(array):
    return lax.ppermute(array, "xc", [(n ^ 1, n) for n in range(8)])


def trade(array):
    return lax.all_to_all(array, "yz", split_axis=0, concat_axis=0, tiled=True, axis_index_groups=TRADERS)


def on_device(queries, keys, values):
    z, xc = lax.axis_index("yz") % 4, lax.axis_index("xc")
    kv = prepare(keys, values)
    own = lax.all_to_all(kv, "yz", split_axis=0, concat_axis=0, tiled=True)
    q = by_head(queries).reshape(8, CHUNK, HEAD_DIM)
    q, own = lax.optimization_barrier((q, own))
    own = own.reshape(4, 4, 2, TOK, HEAD_DIM)
    other = swap(own)
    q = trade(after(q, own[0, 0, 0, :16])).reshape(4, PAIR, HEAD_DIM)
    inner = (z == 1) | (z == 2)
    half = around(jnp.where(inner, own[2:], own[:2]), 2)
    rest = across(half)
    near = [around(own, step) for step in (1, 3)]
    near[0], near[1], rest = lax.optimization_barrier((near[0], near[1], rest))
    far = jnp.concatenate([jnp.where(inner, rest, half), jnp.where(inner, half, rest)], axis=0)
    blocks, slots = [own, other], [xc, xc ^ 1]
    for step, block in ((1, near[0]), (3, near[1]), (2, far)):
        blocks += [block, swap(block)]
        slots += [(xc + 2 * step) % 8, (xc + 2 * step) % 8 ^ 1]
    where = jnp.stack([jnp.where(inner, 1, 0), xc] + slots).astype(jnp.int32)
    out = trade(attend(where, q, blocks))
    return out.transpose(1, 0, 2).reshape(queries.shape)


def solution(mesh):
    fine = Mesh(mesh.devices.reshape(tuple(SIZES.values())), tuple(SIZES))
    spec = P(tuple(SIZES), None)
    return jax.shard_map(
        on_device, mesh=fine, in_specs=(spec,) * 3, out_specs=spec, check_vma=False
    )
```
